32 devices in a mesh: tok: 8 (over z, y), head: 4 (over x, core).
Axes of the slice: x: 2, y: 2, z: 4, core: 2. Of those that a mesh axis runs over, the one named last changes fastest.
Arguments:
- latents: float32 [512, 4096], P(None, 'tok'), may hold values from -6 to 6
- doc_keys: bfloat16 [2048, 4096], P('tok', 'head'), may hold values from -500 to 500
- doc_values: bfloat16 [2048, 4096], P('tok', 'head'), may hold values from -6 to 6
- token_mask: int32 [2048], P('tok'), may hold values from 0 to 1, as said below
- shard_lengths: int32 [8], P('tok'), may hold values from 64 to 256, as said below
- query_weight: bfloat16 [4096, 4096], P('tok', 'head'), may hold values from -0.375 to 0.375
- output_weight: bfloat16 [4096, 4096], P('head', 'tok'), may hold values from -0.375 to 0.375
- attn_gain: float32 [4096], P('tok'), may hold values from 0.1 to 1.9
- up_weight: bfloat16 [4096, 4096], P('tok', 'head'), may hold values from -0.1875 to 0.1875
- down_weight: bfloat16 [4096, 4096], P('head', 'tok'), may hold values from -0.1875 to 0.1875
- mlp_gain: float32 [4096], P('tok'), may hold values from 0.1 to 1.9
Outputs:
- encoded: float32 [512, 4096], P(None, 'tok')
The draws below stay inside these ranges and needn't reach their ends.
Inputs may be any that keep to these rules, and one draw needn't show every extreme that they name: `token_mask`: the first token of every aligned block of 256 tokens is 1. Entry j bounds the valid tokens of block j to its first shard_lengths[j]; some entry equals 256.
All inputs are finite; a program needn't handle non-finite values.
Results may differ from the reference program's by a relative error of at most 0.0035.
The reference program's roundings to bfloat16 on the way count: a program that leaves them out, or rounds other values in their place, can miss the bound.
Values may be sent and summed in bfloat16 or wider, within the bound.
A program may use at most 64 MiB of HBM per device.

```python
import jax
import jax.numpy as jnp
from jax import lax

D = 4096
H = 32
HS = 128
L = 512
FF = 4096
ITERS = 1
TOK_DEV = 256
HD = 4096
TOKENS = 2048
N_TOK = 8


def draw_token_mask(key, part):
    quarter_draw = jax.random.randint(key, (TOKENS,), 0, 4)
    leading = jnp.arange(TOKENS) % TOK_DEV == 0
    return jnp.where(leading | (quarter_draw != 0), 1, 0).astype(jnp.int32)


def draw_shard_lengths(key, part):
    lengths_drawn = jax.random.randint(key, (N_TOK,), TOK_DEV // 4, TOK_DEV + 1)
    full_shard = jax.random.randint(jax.random.fold_in(key, 7), (), 0, N_TOK)
    return jnp.where(jnp.arange(N_TOK) == full_shard, TOK_DEV, lengths_drawn).astype(jnp.int32)


def draw_doc_keys(key, part):
    basic_draw = jax.random.truncated_normal(key, -6.0, 6.0, (TOKENS, HD), jnp.float32)
    return basic_draw.astype(jnp.bfloat16)


def block_scale(rng, shape, pieces, least, top_value):
    level = 1.0
    for axis_at, blocks in pieces:
        draws = jax.random.uniform(jax.random.fold_in(jax.random.fold_in(rng, 6), axis_at), (blocks,), jnp.float32, least / len(pieces), top_value / len(pieces))
        level = level * jnp.repeat(jnp.exp(draws), shape[axis_at] // blocks).reshape((-1,) + (1,) * (len(shape) - 1 - axis_at))
    return level


def normal_values(stream_key, dims, width, bound, cuts=(), held_as=jnp.bfloat16):
    drawn = width * jax.random.normal(stream_key, dims, jnp.float32)
    if cuts:
        drawn = drawn * block_scale(stream_key, dims, cuts, -0.22, 0.18)
    return jnp.clip(drawn, -bound, bound).astype(held_as)


def setup_inputs(seed: int = 0) -> dict:
    keys = jax.random.split(jax.random.key(seed), 12)
    return {
        "latents": normal_values(keys[0], (L, D), 1.0, 6.0, ((1, 8),), jnp.float32),
        "doc_keys": draw_doc_keys(jax.random.fold_in(keys[11], 71), 0),
        "doc_values": normal_values(keys[2], (TOKENS, HD), 1.0, 6.0, ((0, 8), (1, 4))),
        "token_mask": draw_token_mask(jax.random.fold_in(keys[11], 71), 0),
        "shard_lengths": draw_shard_lengths(jax.random.fold_in(keys[11], 71), 0),
        "query_weight": normal_values(keys[5], (D, HD), (D // 16) ** -0.5, 0.375, ((0, 8), (1, 4))),
        "output_weight": normal_values(keys[6], (HD, D), (HD // 16) ** -0.5, 0.375, ((0, 4), (1, 8))),
        "attn_gain": jnp.clip(1.0 + 0.18 * jax.random.normal(keys[7], (D,), jnp.float32), 0.1, 1.9),
        "up_weight": normal_values(keys[8], (D, FF), (D // 4) ** -0.5, 0.1875, ((0, 8), (1, 4))),
        "down_weight": normal_values(keys[9], (FF, D), (FF // 4) ** -0.5, 0.1875, ((0, 4), (1, 8))),
        "mlp_gain": jnp.clip(1.0 + 0.18 * jax.random.normal(keys[10], (D,), jnp.float32), 0.1, 1.9),
    }


epsilon = 1e-05
masked_score = -1e+30

def projected(state, gain, weight):
    scaled = (state * gain).astype(jnp.bfloat16)
    squares = lax.optimization_barrier(jnp.sum(state * state, axis=1))
    inverse = lax.rsqrt(squares / D + epsilon)
    return jnp.dot(scaled, weight, preferred_element_type=jnp.float32) * inverse[:, None]

def combine(left_part, right_part):
    left_top, left_total, left_sum = left_part
    right_top, right_total, right_sum = right_part
    ceiling = jnp.maximum(left_top, right_top)
    left_factor = jnp.exp(left_top - ceiling)
    right_factor = jnp.exp(right_top - ceiling)
    total = left_total * left_factor + right_total * right_factor
    summed = left_sum * left_factor[:, :, None] + right_sum * right_factor[:, :, None]
    return (ceiling, total, summed)

def reference(latents, doc_keys, doc_values, token_mask, shard_lengths, query_weight, output_weight, attn_gain, up_weight, down_weight, mlp_gain):
    score_scale = HS ** (-0.5)
    positions = jnp.arange(TOK_DEV, dtype=jnp.int32)
    valid = (token_mask.reshape(N_TOK, TOK_DEV) == 1) & (positions[None, :] < shard_lengths[:, None])
    key_blocks = doc_keys.reshape(N_TOK, TOK_DEV, H, HS)
    value_blocks = doc_values.reshape(N_TOK, TOK_DEV, H, HS)
    state = latents
    for iteration in range(ITERS):
        queries = projected(state, attn_gain, query_weight).astype(jnp.bfloat16)
        query_heads = queries.reshape(L, H, HS).astype(jnp.float32)

        def shard_step(carry, block):
            key_block, value_block, valid_block = block
            scores = jnp.einsum('lhd,thd->lht', query_heads, key_block.astype(jnp.float32)) * score_scale
            scores = jnp.where(valid_block[None, None, :], scores, masked_score)
            highest = lax.optimization_barrier(jnp.max(scores, axis=2))
            weights = jnp.exp(scores - highest[:, :, None])
            total = lax.optimization_barrier(jnp.sum(weights, axis=2))
            weighted = jnp.einsum('lht,thd->lhd', weights.astype(jnp.bfloat16).astype(jnp.float32), value_block.astype(jnp.float32))
            return (combine(carry, (highest, total, weighted)), None)
        start = (jnp.full((L, H), masked_score, jnp.float32), jnp.zeros((L, H), jnp.float32), jnp.zeros((L, H, HS), jnp.float32))
        merged, unused = lax.scan(shard_step, start, (key_blocks, value_blocks, valid))
        attended = (merged[2] / merged[1][:, :, None]).astype(jnp.bfloat16).reshape(L, HD)
        state = state + jnp.dot(attended, output_weight, preferred_element_type=jnp.float32)
    hidden = jax.nn.gelu(projected(state, mlp_gain, up_weight)).astype(jnp.bfloat16)
    return state + jnp.dot(hidden, down_weight, preferred_element_type=jnp.float32)
```

```python
import functools

import jax
import jax.numpy as jnp
from jax import lax
from jax.experimental import pallas as pl
from jax.experimental.pallas import tpu as pltpu
from jax.sharding import PartitionSpec as P

HS = 128
epsilon = 1e-05
masked_score = -1e30
MESH = pl.DeviceIdType.MESH
f32 = jnp.float32
bf16 = jnp.bfloat16
RS_TYPES = (f32, f32, bf16)
UNROLL = 8


def chunk_count(latent_count, nz):
    count = 1
    while (
        latent_count % (2 * count) == 0
        and latent_count // (2 * count) >= 128
        and latent_count // (2 * count) // nz >= 16
    ):
        count *= 2
    return count


def each(first, last, body):
    if last - first <= UNROLL:
        for d in range(first, last):
            body(d)
    else:

        @pl.loop(first, last)
        def _(d):
            body(d)


def kernel(
    n_tok, n_head, chunks, width,
    lat_ref, key_ref, val_ref, bias_ref, gain_ref, mgain_ref,
    qw_hbm, ow_hbm, uw_hbm, dw_hbm,
    out_ref,
    qw, ow, uw, dw, vt,
    s1_0, s1_1, s1_2, r1_0, r1_1, r1_2, a_0, a_1, a_2, s2_0, s2_1, s2_2, q2_0, q2_1, q2_2,
    g_0, g_1, g_2,
    sq_s, sq_r, st_s, st_r, wt, fac_ref, inv_ref,
    h1s, h1r, h2, state_ref,
    w_sem, c_send, c_recv, t_send, t_recv, h_send, h_recv,
):
    tok = lax.axis_index("tok")
    head = lax.axis_index("head")
    nz = n_tok // 2
    nq = n_head // 2
    z = tok // 2
    b = tok % 2
    hq = head // 2
    hb = head % 2
    rows = lat_ref.shape[0] // chunks
    rg = rows // nz
    hr = rows // 2
    ch = key_ref.shape[1] // 2
    heads = key_ref.shape[1] // HS
    hh_n = heads // 2
    dt = lat_ref.shape[1]
    s1, r1, acc, s2, q2, g = (
        (s1_0, s1_1, s1_2), (r1_0, r1_1, r1_2), (a_0, a_1, a_2), (s2_0, s2_1, s2_2),
        (q2_0, q2_1, q2_2), (g_0, g_1, g_2),
    )
    drains = []

    def zpeer(d):
        return lax.rem(z + d, nz)

    def zfrom(d):
        return lax.rem(z + nz - d, nz)

    def to_tok(src, dst, ss, rs, t):
        return pltpu.make_async_remote_copy(
            src_ref=src, dst_ref=dst, send_sem=ss, recv_sem=rs,
            device_id=(t, head), device_id_type=MESH,
        )

    def to_head(src, dst, ss, rs, h):
        return pltpu.make_async_remote_copy(
            src_ref=src, dst_ref=dst, send_sem=ss, recv_sem=rs,
            device_id=(tok, h), device_id_type=MESH,
        )

    pair = 2 * z + (1 - b)
    hpair = 2 * hq + (1 - hb)

    weights = [
        pltpu.make_async_copy(src, dst, w_sem.at[i])
        for i, (src, dst) in enumerate(((qw_hbm, qw), (ow_hbm, ow), (uw_hbm, uw), (dw_hbm, dw)))
    ]
    for w in weights:
        w.start()

    barrier = pltpu.get_barrier_semaphore()

    def greet(t, h):
        pl.semaphore_signal(barrier, inc=1, device_id=(t, h), device_id_type=MESH)

    each(1, n_tok, lambda d: greet(lax.rem(tok + d, n_tok), head))
    each(1, nq, lambda d: greet(tok, 2 * lax.rem(hq + d, nq) + hb))
    greet(tok, hpair)
    pl.semaphore_wait(barrier, n_tok - 1 + nq)

    def started(make, first, last):
        each(first, last, lambda d: make(d).start())
        drains.append(lambda: each(first, last, lambda d: make(d).wait_send()))

    def pair_send(k, c):
        return to_tok(s1[k].at[c], r1[k].at[c], c_send.at[k, c, 0, 0], c_recv.at[k, c, 0, 0], pair)

    def group_send(k, c, d):
        src = acc[k] if s2[k].shape[0] != chunks else s2[k]
        return to_tok(
            src.at[c, pl.ds(zpeer(d) * rg, rg), :], q2[k].at[c, d],
            c_send.at[k, c, 1, d], c_recv.at[k, c, 1, d], 2 * zpeer(d) + b,
        )

    def share_send(k, c, d):
        at = g[k].at[c, b, pl.ds(z * rg, rg), :]
        return to_tok(at, at, c_send.at[k, c, 2, d], c_recv.at[k, c, 2, d], 2 * zpeer(d) + b)

    def share_recv(k, c, d):
        at = g[k].at[c, b, pl.ds(zfrom(d) * rg, rg), :]
        return to_tok(at, at, c_send.at[k, c, 2, d], c_recv.at[k, c, 2, d], 2 * zpeer(d) + b)

    def cross_send(k, c, d):
        at = g[k].at[c, b, pl.ds(zfrom(d) * rg, rg), :]
        return to_tok(at, at, c_send.at[k, c, 3, d], c_recv.at[k, c, 3, d], pair)

    def cross_recv(k, c, d):
        at = g[k].at[c, 1 - b, pl.ds(zfrom(d) * rg, rg), :]
        return to_tok(at, at, c_send.at[k, c, 3, d], c_recv.at[k, c, 3, d], pair)

    def sum_pair(k, c):
        pair_send(k, c).wait_recv()
        total = acc[k][c] + r1[k][c].astype(f32)
        acc[k][c] = total
        if s2[k].shape[0] == chunks:
            s2[k][c] = total.astype(s2[k].dtype)
        started(functools.partial(group_send, k, c), 1, nz)

    def sum_groups(k, c, finish):
        each(1, nz, lambda d: group_send(k, c, d).wait_recv())
        total = acc[k][c, pl.ds(z * rg, rg), :]
        for d in range(1, nz):
            total = total + q2[k][c, d].astype(f32)
        g[k][c, b, pl.ds(z * rg, rg), :] = finish(total)
        started(functools.partial(share_send, k, c), 1, nz)
        started(functools.partial(cross_send, k, c), 0, 1)

    def forward(k, c):
        def one(d):
            share_recv(k, c, d).wait_recv()
            cross_send(k, c, d).start()

        each(1, nz, one)
        drains.append(lambda: each(1, nz, lambda d: cross_send(k, c, d).wait_send()))

    def gathered(k, c):
        each(0, nz, lambda d: cross_recv(k, c, d).wait_recv())

    def note_send(i, src, dst, c, d):
        return to_tok(
            src, dst.at[d], t_send.at[i, c, d], t_recv.at[i, c, d], lax.rem(tok + d, n_tok)
        )

    def squares_send(k, c, d):
        return note_send(k, sq_s.at[k, c], sq_r.at[k, c], c, d)

    def stats_send(c, d):
        return note_send(2, st_s.at[c], st_r.at[c], c, d)

    def project(k, n, c, state, gain, weight):
        squares = jnp.sum(state * state, axis=1, keepdims=True)
        sq_s[k, c] = jnp.broadcast_to(squares, (rows, 128)).T[0:8, :]
        started(functools.partial(squares_send, k, c), 1, n_tok)
        scaled = (state * gain).astype(bf16)
        tile = min(256, ch)
        for j in range(0, ch, tile):
            part = jnp.dot(
                scaled, weight[:, pl.ds((1 - b) * ch + j, tile)], preferred_element_type=f32
            )
            s1[n][c, :, j : j + tile] = part.astype(s1[n].dtype)
        started(lambda d: pair_send(n, c), 0, 1)
        for j in range(0, ch, tile):
            acc[n][c, :, j : j + tile] = jnp.dot(
                scaled, weight[:, pl.ds(b * ch + j, tile)], preferred_element_type=f32
            )

    def scale_rows(k, c, total):
        each(1, n_tok, lambda d: squares_send(k, c, d).wait_recv())
        squares = sq_s[k, c]
        for d in range(1, n_tok):
            squares = squares + sq_r[k, c, d]
        inverse = lax.rsqrt(squares / width + epsilon)
        inv_ref[...] = jnp.broadcast_to(inverse[0:1, :], (128, rows)).T
        mine = inv_ref[pl.ds(z * rg, rg), :]
        return total * jnp.concatenate([mine] * (ch // 128), axis=1)

    def attend(c):
        for hh in range(hh_n):
            for half in range(2):
                h = half * hh_n + hh
                query = g[0][c, half, :, hh * HS : (hh + 1) * HS]
                scores = lax.dot_general(
                    key_ref[:, h * HS : (h + 1) * HS], query, (((1,), (1,)), ((), ())),
                    preferred_element_type=f32,
                ) * HS ** (-0.5)
                scores = jnp.where(
                    jnp.concatenate([bias_ref[...]] * (rows // 128), axis=1) > 0.5,
                    scores, masked_score,
                )
                highest = jnp.max(scores, axis=0, keepdims=True)
                weights_b = jnp.exp(scores - highest)
                st_s[c, h : h + 1, :] = highest
                st_s[c, heads + h : heads + h + 1, :] = jnp.sum(weights_b, axis=0, keepdims=True)
                wt[c, h] = jnp.dot(
                    vt[h * HS : (h + 1) * HS, :], weights_b.astype(bf16), preferred_element_type=f32
                )
        started(functools.partial(stats_send, c), 1, n_tok)

    def normalise(c):
        each(1, n_tok, lambda d: stats_send(c, d).wait_recv())
        mine = st_s[c]
        top = mine[0:heads]
        for d in range(1, n_tok):
            top = jnp.maximum(top, st_r[c, d, 0:heads, :])
        own = jnp.exp(mine[0:heads] - top)
        den = own * mine[heads:]
        for d in range(1, n_tok):
            den = den + jnp.exp(st_r[c, d, 0:heads, :] - top) * st_r[c, d, heads : 2 * heads, :]
        fac_ref[...] = own / den
        for hh in range(hh_n):
            h = (1 - b) * hh_n + hh
            part = (wt[c, h] * fac_ref[pl.ds(h, 1), :]).T
            s1[1][c, :, hh * HS : (hh + 1) * HS] = part.astype(s1[1].dtype)
        started(lambda d: pair_send(1, c), 0, 1)
        for hh in range(hh_n):
            h = b * hh_n + hh
            acc[1][c, :, hh * HS : (hh + 1) * HS] = (wt[c, h] * fac_ref[pl.ds(h, 1), :]).T

    def hpair_send(m, c):
        return to_head(
            h1s.at[m, c, pl.ds((1 - hb) * hr, hr), :], h1r.at[m, c],
            h_send.at[m, c, 0, 0], h_recv.at[m, c, 0, 0], hpair,
        )

    def hdirect_send(m, c, d):
        at = h2.at[m, c, hq]
        return to_head(
            at, at, h_send.at[m, c, 1, d], h_recv.at[m, c, 1, d], 2 * lax.rem(hq + d, nq) + hb
        )

    def hdirect_recv(m, c, d):
        at = h2.at[m, c, lax.rem(hq + nq - d, nq)]
        return to_head(
            at, at, h_send.at[m, c, 1, d], h_recv.at[m, c, 1, d], 2 * lax.rem(hq + d, nq) + hb
        )

    def hback(m, c, half):
        at = (state_ref if m == 0 else out_ref).at[pl.ds(c * rows + half * hr, hr), :]
        return to_head(at, at, h_send.at[m, c, 2, 0], h_recv.at[m, c, 2, 0], hpair)

    def head_partial(m, c, k, weight):
        tile = min(256, dt)
        left, right = g[k][c, 0], g[k][c, 1]
        for j in range(0, dt, tile):
            h1s[m, c, :, j : j + tile] = jnp.dot(
                left, weight[0:ch, j : j + tile], preferred_element_type=f32
            ) + jnp.dot(right, weight[ch : 2 * ch, j : j + tile], preferred_element_type=f32)
        started(lambda d: hpair_send(m, c), 0, 1)

    def head_pair(m, c):
        hpair_send(m, c).wait_recv()
        h2[m, c, hq] = h1s[m, c, pl.ds(hb * hr, hr), :] + h1r[m, c]
        started(functools.partial(hdirect_send, m, c), 1, nq)

    def head_total(m, c):
        each(1, nq, lambda d: hdirect_recv(m, c, d).wait_recv())
        total = h2[m, c, 0]
        for i in range(1, nq):
            total = total + h2[m, c, i]
        at = pl.ds(c * rows + hb * hr, hr)
        if m == 0:
            state_ref[at, :] = lat_ref[at, :] + total
        else:
            out_ref[at, :] = state_ref[at, :] + total
        started(lambda d: hback(m, c, hb), 0, 1)

    def head_back(m, c):
        hback(m, c, 1 - hb).wait_recv()

    def stage_0(c):
        if c == 0:
            weights[0].wait()
        project(0, 0, c, lat_ref[c * rows : (c + 1) * rows, :], gain_ref[...], qw)
        if c == chunks - 1:
            for h in range(heads):
                vt[h * HS : (h + 1) * HS, :] = (
                    val_ref[:, h * HS : (h + 1) * HS].astype(f32).T.astype(bf16)
                )

    def stage_2(c):
        sum_groups(0, c, lambda t: scale_rows(0, c, t).astype(bf16))

    def stage_4(c):
        gathered(0, c)
        attend(c)

    def stage_9(c):
        if c == 0:
            weights[1].wait()
        gathered(1, c)
        head_partial(0, c, 1, ow)

    def stage_12(c):
        if c == 0:
            weights[2].wait()
        head_back(0, c)
        project(1, 2, c, state_ref[c * rows : (c + 1) * rows, :], mgain_ref[...], uw)

    def pair_2(c):
        sum_pair(2, c)

    def stage_14(c):
        sum_groups(2, c, lambda t: jax.nn.gelu(scale_rows(1, c, t)).astype(bf16))

    def stage_16(c):
        if c == 0:
            weights[3].wait()
        gathered(2, c)
        head_partial(1, c, 2, dw)

    stages = [
        stage_0,
        lambda c: sum_pair(0, c),
        stage_2,
        lambda c: forward(0, c),
        stage_4,
        normalise,
        lambda c: sum_pair(1, c),
        lambda c: sum_groups(1, c, lambda t: t.astype(bf16)),
        lambda c: forward(1, c),
        stage_9,
        lambda c: head_pair(0, c),
        lambda c: head_total(0, c),
        stage_12,
        pair_2,
        stage_14,
        lambda c: forward(2, c),
        stage_16,
        lambda c: head_pair(1, c),
        lambda c: head_total(1, c),
        lambda c: head_back(1, c),
    ]
    for step in range(len(stages) + chunks - 1):
        for c in range(chunks):
            if 0 <= step - c < len(stages):
                stages[step - c](c)
    for drain in drains:
        drain()


def shards(
    n_tok, n_head, latents, doc_keys, doc_values, token_mask, shard_lengths,
    query_weight, output_weight, attn_gain, up_weight, down_weight, mlp_gain,
):
    token_count, features = doc_keys.shape
    latent_count, dt = latents.shape
    positions = jnp.arange(token_count, dtype=jnp.int32)
    valid = (token_mask == 1) & (positions < shard_lengths[0])
    bias = jnp.broadcast_to(valid.astype(f32)[:, None], (token_count, 128))
    nz, nq = n_tok // 2, n_head // 2
    chunks = chunk_count(latent_count, nz)
    rows = latent_count // chunks
    rg, ch, heads = rows // nz, features // 2, features // HS

    def per(make):
        return [make(t) for t in RS_TYPES]

    scratch = [
        pltpu.VMEM(query_weight.shape, bf16), pltpu.VMEM(output_weight.shape, bf16),
        pltpu.VMEM(up_weight.shape, bf16), pltpu.VMEM(down_weight.shape, bf16),
        pltpu.VMEM((features, token_count), bf16),
        *per(lambda t: pltpu.VMEM((chunks, rows, ch), t)),
        *per(lambda t: pltpu.VMEM((chunks, rows, ch), t)),
        *per(lambda t: pltpu.VMEM((chunks, rows, ch), f32)),
        *per(lambda t: pltpu.VMEM((chunks, rows, ch) if t != f32 else (chunks + 1, 8, 128), t)),
        *per(lambda t: pltpu.VMEM((chunks, nz, rg, ch), t)),
        *per(lambda t: pltpu.VMEM((chunks, 2, rows, ch), bf16)),
        pltpu.VMEM((2, chunks, 8, rows), f32),
        pltpu.VMEM((2, chunks, n_tok, 8, rows), f32),
        pltpu.VMEM((chunks, 2 * heads, rows), f32),
        pltpu.VMEM((chunks, n_tok, 2 * heads, rows), f32),
        pltpu.VMEM((chunks, heads, HS, rows), f32),
        pltpu.VMEM((heads, rows), f32),
        pltpu.VMEM((rows, 128), f32),
        pltpu.VMEM((2, chunks, rows, dt), f32),
        pltpu.VMEM((2, chunks, rows // 2, dt), f32),
        pltpu.VMEM((2, chunks, nq, rows // 2, dt), f32),
        pltpu.VMEM((latent_count, dt), f32),
        pltpu.SemaphoreType.DMA((4,)),
        pltpu.SemaphoreType.DMA((3, chunks, 4, nz)),
        pltpu.SemaphoreType.DMA((3, chunks, 4, nz)),
        pltpu.SemaphoreType.DMA((3, chunks, n_tok)),
        pltpu.SemaphoreType.DMA((3, chunks, n_tok)),
        pltpu.SemaphoreType.DMA((2, chunks, 3, nq)),
        pltpu.SemaphoreType.DMA((2, chunks, 3, nq)),
    ]
    vmem = pl.BlockSpec(memory_space=pltpu.VMEM)
    anywhere = pl.BlockSpec(memory_space=pl.ANY)
    return pl.pallas_call(
        functools.partial(kernel, n_tok, n_head, chunks, dt * n_tok),
        out_shape=jax.ShapeDtypeStruct(latents.shape, f32),
        in_specs=[vmem] * 6 + [anywhere] * 4,
        out_specs=vmem,
        scratch_shapes=scratch,
        compiler_params=pltpu.CompilerParams(
            collective_id=0, has_side_effects=True, vmem_limit_bytes=56 * 1024 * 1024
        ),
    )(
        latents, doc_keys, doc_values, bias, attn_gain[None, :], mlp_gain[None, :],
        query_weight, output_weight, up_weight, down_weight,
    )


def solution(mesh):
    in_specs = (
        P(None, "tok"),
        P("tok", "head"),
        P("tok", "head"),
        P("tok"),
        P("tok"),
        P("tok", "head"),
        P("head", "tok"),
        P("tok"),
        P("tok", "head"),
        P("head", "tok"),
        P("tok"),
    )
    return jax.shard_map(
        functools.partial(shards, mesh.shape["tok"], mesh.shape["head"]),
        mesh=mesh, in_specs=in_specs, out_specs=P(None, "tok"), check_vma=False,
    )
```

```python
import functools

import jax
import jax.numpy as jnp
from jax import lax
from jax.experimental import pallas as pl
from jax.experimental.pallas import tpu as pltpu
from jax.sharding import PartitionSpec as P

HS = 128
epsilon = 1e-05
masked_score = -1e30
MESH = pl.DeviceIdType.MESH
f32 = jnp.float32
bf16 = jnp.bfloat16
RS_TYPES = (f32, jnp.int16, bf16)
FULL = 32000.0
KV_AT = 1
SKEW = 1
UNROLL = 8


def chunk_count(latent_count, nz):
    count = 1
    while (
        latent_count % (2 * count) == 0
        and latent_count // (2 * count) >= 128
        and latent_count // (2 * count) // nz >= 16
    ):
        count *= 2
    return count


def each(first, last, body):
    if last - first <= UNROLL:
        for d in range(first, last):
            body(d)
    else:

        @pl.loop(first, last)
        def _(d):
            body(d)


def kernel(
    n_tok, n_head, chunks, width,
    lat_ref, key_ref, val_ref, bias_ref, gain_ref, mgain_ref,
    qw_hbm, ow_hbm, uw_hbm, dw_hbm,
    out_ref,
    qw, ow, uw, dw, vt,
    s1_0, s1_1, s1_2, r1_0, r1_1, r1_2, a_0, a_1, a_2, s2_0, s2_1, s2_2, q2_0, q2_1, q2_2,
    g_0, g_1, g_2,
    sq_s, sq_r, st_s, st_r, wt, inv_ref, k2, v2, bias2, mask, scale_ref,
    h1s, h1r, h2, state_ref,
    w_sem, c_send, c_recv, t_send, t_recv, h_send, h_recv, kv_send, kv_recv,
):
    tok = lax.axis_index("tok")
    head = lax.axis_index("head")
    nz = n_tok // 2
    nq = n_head // 2
    z = tok // 2
    b = tok % 2
    hq = head // 2
    hb = head % 2
    rows = lat_ref.shape[0] // chunks
    rg = rows // nz
    hr = rows // 2
    ch = key_ref.shape[1] // 2
    hh_n = ch // HS
    token_count = key_ref.shape[0]
    dt = lat_ref.shape[1]
    s1, r1, acc, s2, q2, g = (
        (s1_0, s1_1, s1_2), (r1_0, r1_1, r1_2), (a_0, a_1, a_2), (s2_0, s2_1, s2_2),
        (q2_0, q2_1, q2_2), (g_0, g_1, g_2),
    )
    drains = []

    def zpeer(d):
        return lax.rem(z + d, nz)

    def zfrom(d):
        return lax.rem(z + nz - d, nz)

    def to_tok(src, dst, ss, rs, t):
        return pltpu.make_async_remote_copy(
            src_ref=src, dst_ref=dst, send_sem=ss, recv_sem=rs,
            device_id=(t, head), device_id_type=MESH,
        )

    def to_head(src, dst, ss, rs, h):
        return pltpu.make_async_remote_copy(
            src_ref=src, dst_ref=dst, send_sem=ss, recv_sem=rs,
            device_id=(tok, h), device_id_type=MESH,
        )

    pair = 2 * z + (1 - b)
    hpair = 2 * hq + (1 - hb)

    weights = [
        pltpu.make_async_copy(src, dst, w_sem.at[i])
        for i, (src, dst) in enumerate(((qw_hbm, qw), (ow_hbm, ow), (uw_hbm, uw), (dw_hbm, dw)))
    ]
    for w in weights:
        w.start()

    barrier = pltpu.get_barrier_semaphore()

    def greet(t, h):
        pl.semaphore_signal(barrier, inc=1, device_id=(t, h), device_id_type=MESH)

    each(1, n_tok, lambda d: greet(lax.rem(tok + d, n_tok), head))
    each(1, nq, lambda d: greet(tok, 2 * lax.rem(hq + d, nq) + hb))
    greet(tok, hpair)
    pl.semaphore_wait(barrier, n_tok - 1 + nq)

    def started(make, first, last):
        each(first, last, lambda d: make(d).start())
        drains.append(lambda: each(first, last, lambda d: make(d).wait_send()))

    def pair_send(k, c):
        return to_tok(s1[k].at[c], r1[k].at[c], c_send.at[k, c, 0, 0], c_recv.at[k, c, 0, 0], pair)

    def group_send(k, c, d):
        src = acc[k] if s2[k].shape[0] != chunks else s2[k]
        return to_tok(
            src.at[c, pl.ds(zpeer(d) * rg, rg), :], q2[k].at[c, d],
            c_send.at[k, c, 1, d], c_recv.at[k, c, 1, d], 2 * zpeer(d) + b,
        )

    def share_send(k, c, d):
        at = g[k].at[c, b, pl.ds(z * rg, rg), :]
        return to_tok(at, at, c_send.at[k, c, 2, d], c_recv.at[k, c, 2, d], 2 * zpeer(d) + b)

    def share_recv(k, c, d):
        at = g[k].at[c, b, pl.ds(zfrom(d) * rg, rg), :]
        return to_tok(at, at, c_send.at[k, c, 2, d], c_recv.at[k, c, 2, d], 2 * zpeer(d) + b)

    def cross_send(k, c, d):
        at = g[k].at[c, b, pl.ds(zfrom(d) * rg, rg), :]
        return to_tok(at, at, c_send.at[k, c, 3, d], c_recv.at[k, c, 3, d], pair)

    def cross_recv(k, c, d):
        at = g[k].at[c, 1 - b, pl.ds(zfrom(d) * rg, rg), :]
        return to_tok(at, at, c_send.at[k, c, 3, d], c_recv.at[k, c, 3, d], pair)

    def sum_pair(k, c):
        pair_send(k, c).wait_recv()
        total = acc[k][c] + r1[k][c].astype(f32)
        acc[k][c] = total
        if s2[k].shape[0] == chunks:
            s2[k][c] = total.astype(s2[k].dtype)
        started(functools.partial(group_send, k, c), 1, nz)

    def sum_groups(k, c, finish):
        each(1, nz, lambda d: group_send(k, c, d).wait_recv())
        total = acc[k][c, pl.ds(z * rg, rg), :]
        for d in range(1, nz):
            term = q2[k][c, d].astype(f32)
            if k == 1:
                term = term * jnp.concatenate([scale_ref[c, 1:2, :]] * hh_n, axis=1)
            total = total + term
        g[k][c, b, pl.ds(z * rg, rg), :] = finish(total)
        started(functools.partial(share_send, k, c), 1, nz)
        if k > 0:
            started(functools.partial(cross_send, k, c), 0, 1)

    def forward(k, c):
        def one(d):
            share_recv(k, c, d).wait_recv()
            cross_send(k, c, d).start()

        each(1, nz, one)
        drains.append(lambda: each(1, nz, lambda d: cross_send(k, c, d).wait_send()))

    def gathered(k, c):
        each(0, nz, lambda d: cross_recv(k, c, d).wait_recv())

    def note_send(i, src, dst, c, d, t):
        return to_tok(src, dst.at[d], t_send.at[i, c, d], t_recv.at[i, c, d], t)

    def squares_send(k, c, d):
        return note_send(k, sq_s.at[k, c], sq_r.at[k, c], c, d, lax.rem(tok + d, n_tok))

    def stats_send(c, d):
        return note_send(2, st_s.at[c], st_r.at[c], c, d, 2 * zpeer(d) + b)

    def project(k, n, c, state, gain, weight):
        squares = jnp.sum(state * state, axis=1, keepdims=True)
        sq_s[k, c] = jnp.broadcast_to(squares, (rows, 128)).T[0:8, :]
        started(functools.partial(squares_send, k, c), 1, n_tok)
        scaled = (state * gain).astype(bf16)
        tile = min(256, ch)
        for j in range(0, ch, tile):
            part = jnp.dot(
                scaled, weight[:, pl.ds((1 - b) * ch + j, tile)], preferred_element_type=f32
            )
            s1[n][c, :, j : j + tile] = part.astype(s1[n].dtype)
        started(lambda d: pair_send(n, c), 0, 1)
        for j in range(0, ch, tile):
            acc[n][c, :, j : j + tile] = jnp.dot(
                scaled, weight[:, pl.ds(b * ch + j, tile)], preferred_element_type=f32
            )

    def scale_rows(k, c, total):
        each(1, n_tok, lambda d: squares_send(k, c, d).wait_recv())
        squares = sq_s[k, c]
        for d in range(1, n_tok):
            squares = squares + sq_r[k, c, d]
        inverse = lax.rsqrt(squares / width + epsilon)
        inv_ref[...] = jnp.broadcast_to(inverse[0:1, :], (128, rows)).T
        mine = inv_ref[pl.ds(z * rg, rg), :]
        return total * jnp.concatenate([mine] * (ch // 128), axis=1)

    def doc_sends():
        cols = pl.ds((1 - b) * ch, ch)
        return [
            to_tok(src, dst, kv_send.at[i], kv_recv.at[i], pair)
            for i, (src, dst) in enumerate(
                ((key_ref.at[:, cols], k2), (val_ref.at[:, cols], v2), (bias_ref, bias2))
            )
        ]

    def send_docs():
        for copy in doc_sends():
            copy.start()
        drains.append(lambda: [copy.wait_send() for copy in doc_sends()])

    def receive_docs():
        for copy in doc_sends():
            copy.wait_recv()
        biggest = jnp.zeros((1, 128), f32)
        for i, bias in enumerate((bias_ref, bias2)):
            mask[i] = jnp.broadcast_to(bias[0:1, :], (128, token_count)).T
            for hh in range(hh_n):
                if i == 0:
                    piece = val_ref[:, pl.ds(b * ch + hh * HS, HS)]
                else:
                    piece = v2[:, hh * HS : (hh + 1) * HS]
                piece = piece.astype(f32)
                biggest = jnp.maximum(biggest, jnp.max(jnp.abs(piece), axis=0, keepdims=True))
                vt[i, hh * HS : (hh + 1) * HS, :] = piece.T.astype(bf16)
        biggest = jnp.broadcast_to(jnp.max(biggest, axis=1, keepdims=True), (8, rows))
        for c in range(chunks):
            st_s[c, 2 * hh_n : 2 * hh_n + 8, :] = biggest

    def attend(c):
        for hh in range(hh_n):
            query = g[0][c, b, :, hh * HS : (hh + 1) * HS]
            parts = []
            for i in range(2):
                if i == 0:
                    keys = key_ref[:, pl.ds(b * ch + hh * HS, HS)]
                else:
                    keys = k2[:, hh * HS : (hh + 1) * HS]
                scores = lax.dot_general(
                    keys, query, (((1,), (1,)), ((), ())), preferred_element_type=f32
                ) * HS ** (-0.5)
                scores = jnp.where(
                    jnp.concatenate([mask[i]] * (rows // 128), axis=1) > 0.5, scores, masked_score
                )
                highest = jnp.max(scores, axis=0, keepdims=True)
                weights_b = jnp.exp(scores - highest)
                total = jnp.sum(weights_b, axis=0, keepdims=True)
                weighted = jnp.dot(
                    vt[i, hh * HS : (hh + 1) * HS, :], weights_b.astype(bf16),
                    preferred_element_type=f32,
                )
                parts.append((highest, total, weighted))
            (top_0, total_0, sum_0), (top_1, total_1, sum_1) = parts
            top = jnp.maximum(top_0, top_1)
            left, right = jnp.exp(top_0 - top), jnp.exp(top_1 - top)
            st_s[c, hh : hh + 1, :] = top
            st_s[c, hh_n + hh : hh_n + hh + 1, :] = left * total_0 + right * total_1
            wt[c, hh] = sum_0 * left + sum_1 * right
        started(functools.partial(stats_send, c), 1, nz)

    def normalise(c):
        each(1, nz, lambda d: stats_send(c, d).wait_recv())
        mine = st_s[c]
        top, biggest = mine[0:hh_n], mine[2 * hh_n :]
        for d in range(1, nz):
            top = jnp.maximum(top, st_r[c, d, 0:hh_n, :])
            biggest = jnp.maximum(biggest, st_r[c, d, 2 * hh_n :, :])
        own = jnp.exp(mine[0:hh_n] - top)
        den = own * mine[hh_n : 2 * hh_n]
        for d in range(1, nz):
            den = den + jnp.exp(st_r[c, d, 0:hh_n, :] - top) * st_r[c, d, hh_n : 2 * hh_n, :]
        factor = own / den
        biggest = jnp.maximum(biggest[0:1, 0:128], 1e-30)
        scale_ref[c, 0:1, :] = FULL / biggest
        scale_ref[c, 1:2, :] = biggest / FULL
        for hh in range(hh_n):
            part = (wt[c, hh] * factor[hh : hh + 1, :]).T
            acc[1][c, :, hh * HS : (hh + 1) * HS] = part
            s2[1][c, :, hh * HS : (hh + 1) * HS] = (
                jnp.round(part * scale_ref[c, 0:1, :]).astype(jnp.int32).astype(jnp.int16)
            )
        started(functools.partial(group_send, 1, c), 1, nz)

    def hpair_send(m, c):
        return to_head(
            h1s.at[m, c, pl.ds((1 - hb) * hr, hr), :], h1r.at[m, c],
            h_send.at[m, c, 0, 0], h_recv.at[m, c, 0, 0], hpair,
        )

    def hdirect_send(m, c, d):
        at = h2.at[m, c, hq]
        return to_head(
            at, at, h_send.at[m, c, 1, d], h_recv.at[m, c, 1, d], 2 * lax.rem(hq + d, nq) + hb
        )

    def hdirect_recv(m, c, d):
        at = h2.at[m, c, lax.rem(hq + nq - d, nq)]
        return to_head(
            at, at, h_send.at[m, c, 1, d], h_recv.at[m, c, 1, d], 2 * lax.rem(hq + d, nq) + hb
        )

    def hback(m, c, half):
        at = (state_ref if m == 0 else out_ref).at[pl.ds(c * rows + half * hr, hr), :]
        return to_head(at, at, h_send.at[m, c, 2, 0], h_recv.at[m, c, 2, 0], hpair)

    def head_partial(m, c, k, weight):
        tile = min(256, dt)
        left, right = g[k][c, 0], g[k][c, 1]
        for j in range(0, dt, tile):
            h1s[m, c, :, j : j + tile] = jnp.dot(
                left, weight[0:ch, j : j + tile], preferred_element_type=f32
            ) + jnp.dot(right, weight[ch : 2 * ch, j : j + tile], preferred_element_type=f32)
        started(lambda d: hpair_send(m, c), 0, 1)

    def head_pair(m, c):
        hpair_send(m, c).wait_recv()
        h2[m, c, hq] = h1s[m, c, pl.ds(hb * hr, hr), :] + h1r[m, c]
        started(functools.partial(hdirect_send, m, c), 1, nq)

    def head_total(m, c):
        each(1, nq, lambda d: hdirect_recv(m, c, d).wait_recv())
        total = h2[m, c, 0]
        for i in range(1, nq):
            total = total + h2[m, c, i]
        at = pl.ds(c * rows + hb * hr, hr)
        if m == 0:
            state_ref[at, :] = lat_ref[at, :] + total
        else:
            out_ref[at, :] = state_ref[at, :] + total
        started(lambda d: hback(m, c, hb), 0, 1)

    def head_back(m, c):
        hback(m, c, 1 - hb).wait_recv()

    def stage_0(c):
        if c == 0:
            weights[0].wait()
        project(0, 0, c, lat_ref[c * rows : (c + 1) * rows, :], gain_ref[...], qw)
        if c == min(KV_AT, chunks - 1):
            send_docs()

    def stage_2(c):
        sum_groups(0, c, lambda t: scale_rows(0, c, t).astype(bf16))

    def stage_4(c):
        if c == 0:
            receive_docs()
        each(1, nz, lambda d: share_recv(0, c, d).wait_recv())
        attend(c)

    def stage_9(c):
        if c == 0:
            weights[1].wait()
        gathered(1, c)
        head_partial(0, c, 1, ow)

    def stage_12(c):
        if c == 0:
            weights[2].wait()
        head_back(0, c)
        project(1, 2, c, state_ref[c * rows : (c + 1) * rows, :], mgain_ref[...], uw)

    def pair_2(c):
        sum_pair(2, c)

    def stage_14(c):
        sum_groups(2, c, lambda t: jax.nn.gelu(scale_rows(1, c, t)).astype(bf16))

    def stage_16(c):
        if c == 0:
            weights[3].wait()
        gathered(2, c)
        head_partial(1, c, 2, dw)

    stages = [
        stage_0,
        lambda c: sum_pair(0, c),
        stage_2,
        stage_4,
        normalise,
        lambda c: sum_groups(1, c, lambda t: t.astype(bf16)),
        lambda c: forward(1, c),
        stage_9,
        lambda c: head_pair(0, c),
        lambda c: head_total(0, c),
        stage_12,
        pair_2,
        stage_14,
        lambda c: forward(2, c),
        stage_16,
        lambda c: head_pair(1, c),
        lambda c: head_total(1, c),
        lambda c: head_back(1, c),
    ]
    for step in range(len(stages) + SKEW * (chunks - 1)):
        for c in range(chunks):
            if 0 <= step - SKEW * c < len(stages):
                stages[step - SKEW * c](c)
    for drain in drains:
        drain()


def shards(
    n_tok, n_head, latents, doc_keys, doc_values, token_mask, shard_lengths,
    query_weight, output_weight, attn_gain, up_weight, down_weight, mlp_gain,
):
    token_count, features = doc_keys.shape
    latent_count, dt = latents.shape
    positions = jnp.arange(token_count, dtype=jnp.int32)
    valid = (token_mask == 1) & (positions < shard_lengths[0])
    bias = jnp.broadcast_to(valid.astype(f32)[None, :], (8, token_count))
    nz, nq = n_tok // 2, n_head // 2
    chunks = chunk_count(latent_count, nz)
    rows = latent_count // chunks
    rg, ch, hh_n = rows // nz, features // 2, features // (2 * HS)

    def per(make):
        return [make(t) for t in RS_TYPES]

    scratch = [
        pltpu.VMEM(query_weight.shape, bf16), pltpu.VMEM(output_weight.shape, bf16),
        pltpu.VMEM(up_weight.shape, bf16), pltpu.VMEM(down_weight.shape, bf16),
        pltpu.VMEM((2, ch, token_count), bf16),
        *per(lambda t: pltpu.VMEM((chunks, rows, ch), t)),
        *per(lambda t: pltpu.VMEM((chunks, rows, ch), t)),
        *per(lambda t: pltpu.VMEM((chunks, rows, ch), f32)),
        *per(lambda t: pltpu.VMEM((chunks, rows, ch) if t != f32 else (chunks + 1, 8, 128), t)),
        *per(lambda t: pltpu.VMEM((chunks, nz, rg, ch), t)),
        *per(lambda t: pltpu.VMEM((chunks, 2, rows, ch), bf16)),
        pltpu.VMEM((2, chunks, 8, rows), f32),
        pltpu.VMEM((2, chunks, n_tok, 8, rows), f32),
        pltpu.VMEM((chunks, 2 * hh_n + 8, rows), f32),
        pltpu.VMEM((chunks, nz, 2 * hh_n + 8, rows), f32),
        pltpu.VMEM((chunks, hh_n, HS, rows), f32),
        pltpu.VMEM((rows, 128), f32),
        pltpu.VMEM((token_count, ch), bf16),
        pltpu.VMEM((token_count, ch), bf16),
        pltpu.VMEM((8, token_count), f32),
        pltpu.VMEM((2, token_count, 128), f32),
        pltpu.VMEM((chunks, 8, 128), f32),
        pltpu.VMEM((2, chunks, rows, dt), f32),
        pltpu.VMEM((2, chunks, rows // 2, dt), f32),
        pltpu.VMEM((2, chunks, nq, rows // 2, dt), f32),
        pltpu.VMEM((latent_count, dt), f32),
        pltpu.SemaphoreType.DMA((4,)),
        pltpu.SemaphoreType.DMA((3, chunks, 4, nz)),
        pltpu.SemaphoreType.DMA((3, chunks, 4, nz)),
        pltpu.SemaphoreType.DMA((3, chunks, n_tok)),
        pltpu.SemaphoreType.DMA((3, chunks, n_tok)),
        pltpu.SemaphoreType.DMA((2, chunks, 3, nq)),
        pltpu.SemaphoreType.DMA((2, chunks, 3, nq)),
        pltpu.SemaphoreType.DMA((3,)),
        pltpu.SemaphoreType.DMA((3,)),
    ]
    vmem = pl.BlockSpec(memory_space=pltpu.VMEM)
    anywhere = pl.BlockSpec(memory_space=pl.ANY)
    return pl.pallas_call(
        functools.partial(kernel, n_tok, n_head, chunks, dt * n_tok),
        out_shape=jax.ShapeDtypeStruct(latents.shape, f32),
        in_specs=[vmem] * 6 + [anywhere] * 4,
        out_specs=vmem,
        scratch_shapes=scratch,
        compiler_params=pltpu.CompilerParams(
            collective_id=0, has_side_effects=True, vmem_limit_bytes=56 * 1024 * 1024
        ),
    )(
        latents, doc_keys, doc_values, bias, attn_gain[None, :], mlp_gain[None, :],
        query_weight, output_weight, up_weight, down_weight,
    )


def solution(mesh):
    in_specs = (
        P(None, "tok"),
        P("tok", "head"),
        P("tok", "head"),
        P("tok"),
        P("tok"),
        P("tok", "head"),
        P("head", "tok"),
        P("tok"),
        P("tok", "head"),
        P("head", "tok"),
        P("tok"),
    )
    return jax.shard_map(
        functools.partial(shards, mesh.shape["tok"], mesh.shape["head"]),
        mesh=mesh, in_specs=in_specs, out_specs=P(None, "tok"), check_vma=False,
    )
```

```python
import functools

import jax
import jax.numpy as jnp
from jax import lax
from jax.experimental import pallas as pl
from jax.experimental.pallas import tpu as pltpu
from jax.sharding import PartitionSpec as P

HS = 128
epsilon = 1e-05
masked_score = -1e30
MESH = pl.DeviceIdType.MESH
f32 = jnp.float32
bf16 = jnp.bfloat16
RS_TYPES = (f32, jnp.int16, bf16)
FULL = 32000.0

UNROLL = 8


def chunk_count(latent_count, nz):
    count = 1
    while (
        latent_count % (2 * count) == 0
        and latent_count // (2 * count) >= 128
        and latent_count // (2 * count) // nz >= 16
    ):
        count *= 2
    return count


def each(first, last, body):
    if last - first <= UNROLL:
        for d in range(first, last):
            body(d)
    else:

        @pl.loop(first, last)
        def _(d):
            body(d)


def kernel(
    n_tok, n_head, chunks, width,
    lat_ref, key_ref, val_ref, bias_ref, gain_ref, mgain_ref,
    qw_hbm, ow_hbm, uw_hbm, dw_hbm,
    out_ref,
    qw, ow, uw, dw, vt,
    s1_0, s1_1, s1_2, r1_0, r1_1, r1_2, a_0, a_1, a_2, s2_0, s2_1, s2_2, q2_0, q2_1, q2_2,
    g_0, g_1, g_2,
    sq_s, sq_r, st_s, st_r, wt, inv_ref, k2, v2, bias2, mask, scale_ref,
    h1s, h1r, h2, state_ref,
    w_sem, c_send, c_recv, t_send, t_recv, h_send, h_recv, kv_send, kv_recv,
):
    tok = lax.axis_index("tok")
    head = lax.axis_index("head")
    nz = n_tok // 2
    nq = n_head // 2
    z = tok // 2
    b = tok % 2
    hq = head // 2
    hb = head % 2
    rows = lat_ref.shape[0] // chunks
    rg = rows // nz
    hr = rows // 2
    ch = key_ref.shape[1] // 2
    hh_n = ch // HS
    token_count = key_ref.shape[0]
    dt = lat_ref.shape[1]
    s1, r1, acc, s2, q2, g = (
        (s1_0, s1_1, s1_2), (r1_0, r1_1, r1_2), (a_0, a_1, a_2), (s2_0, s2_1, s2_2),
        (q2_0, q2_1, q2_2), (g_0, g_1, g_2),
    )
    drains = []

    def zpeer(d):
        return lax.rem(z + d, nz)

    def zfrom(d):
        return lax.rem(z + nz - d, nz)

    def to_tok(src, dst, ss, rs, t):
        return pltpu.make_async_remote_copy(
            src_ref=src, dst_ref=dst, send_sem=ss, recv_sem=rs,
            device_id=(t, head), device_id_type=MESH,
        )

    def to_head(src, dst, ss, rs, h):
        return pltpu.make_async_remote_copy(
            src_ref=src, dst_ref=dst, send_sem=ss, recv_sem=rs,
            device_id=(tok, h), device_id_type=MESH,
        )

    pair = 2 * z + (1 - b)
    hpair = 2 * hq + (1 - hb)

    weights = [
        pltpu.make_async_copy(src, dst, w_sem.at[i])
        for i, (src, dst) in enumerate(((qw_hbm, qw), (ow_hbm, ow), (uw_hbm, uw), (dw_hbm, dw)))
    ]
    for w in weights:
        w.start()

    barrier = pltpu.get_barrier_semaphore()

    def greet(t, h):
        pl.semaphore_signal(barrier, inc=1, device_id=(t, h), device_id_type=MESH)

    each(1, n_tok, lambda d: greet(lax.rem(tok + d, n_tok), head))
    each(1, nq, lambda d: greet(tok, 2 * lax.rem(hq + d, nq) + hb))
    greet(tok, hpair)
    pl.semaphore_wait(barrier, n_tok - 1 + nq)

    def started(make, first, last):
        each(first, last, lambda d: make(d).start())
        drains.append(lambda: each(first, last, lambda d: make(d).wait_send()))

    def pair_send(k, c):
        return to_tok(s1[k].at[c], r1[k].at[c], c_send.at[k, c, 0, 0], c_recv.at[k, c, 0, 0], pair)

    def group_send(k, c, d):
        src = acc[k] if s2[k].shape[0] != chunks else s2[k]
        return to_tok(
            src.at[c, pl.ds(zpeer(d) * rg, rg), :], q2[k].at[c, d],
            c_send.at[k, c, 1, d], c_recv.at[k, c, 1, d], 2 * zpeer(d) + b,
        )

    def share_send(k, c, d):
        at = g[k].at[c, b, pl.ds(z * rg, rg), :]
        return to_tok(at, at, c_send.at[k, c, 2, d], c_recv.at[k, c, 2, d], 2 * zpeer(d) + b)

    def share_recv(k, c, d):
        at = g[k].at[c, b, pl.ds(zfrom(d) * rg, rg), :]
        return to_tok(at, at, c_send.at[k, c, 2, d], c_recv.at[k, c, 2, d], 2 * zpeer(d) + b)

    def cross_send(k, c, d):
        at = g[k].at[c, b, pl.ds(zfrom(d) * rg, rg), :]
        return to_tok(at, at, c_send.at[k, c, 3, d], c_recv.at[k, c, 3, d], pair)

    def cross_recv(k, c, d):
        at = g[k].at[c, 1 - b, pl.ds(zfrom(d) * rg, rg), :]
        return to_tok(at, at, c_send.at[k, c, 3, d], c_recv.at[k, c, 3, d], pair)

    def sum_pair(k, c):
        pair_send(k, c).wait_recv()
        total = acc[k][c] + r1[k][c].astype(f32)
        acc[k][c] = total
        if s2[k].shape[0] == chunks:
            s2[k][c] = total.astype(s2[k].dtype)
        started(functools.partial(group_send, k, c), 1, nz)

    def sum_groups(k, c, finish):
        each(1, nz, lambda d: group_send(k, c, d).wait_recv())
        total = acc[k][c, pl.ds(z * rg, rg), :]
        for d in range(1, nz):
            term = q2[k][c, d].astype(f32)
            if k == 1:
                term = term * jnp.concatenate([scale_ref[c, 1:2, :]] * hh_n, axis=1)
            total = total + term
        g[k][c, b, pl.ds(z * rg, rg), :] = finish(total)
        started(functools.partial(share_send, k, c), 1, nz)
        if k > 0:
            started(functools.partial(cross_send, k, c), 0, 1)

    def forward(k, c):
        def one(d):
            share_recv(k, c, d).wait_recv()
            cross_send(k, c, d).start()

        each(1, nz, one)
        drains.append(lambda: each(1, nz, lambda d: cross_send(k, c, d).wait_send()))

    def gathered(k, c):
        each(0, nz, lambda d: cross_recv(k, c, d).wait_recv())

    def note_send(i, src, dst, c, d, t):
        return to_tok(src, dst.at[d], t_send.at[i, c, d], t_recv.at[i, c, d], t)

    def squares_send(k, c, d):
        return note_send(k, sq_s.at[k, c], sq_r.at[k, c], c, d, lax.rem(tok + d, n_tok))

    def stats_send(c, d):
        return note_send(2, st_s.at[c], st_r.at[c], c, d, 2 * zpeer(d) + b)

    def project(k, n, c, state, gain, weight):
        squares = jnp.sum(state * state, axis=1, keepdims=True)
        sq_s[k, c] = jnp.broadcast_to(squares, (rows, 128)).T[0:8, :]
        started(functools.partial(squares_send, k, c), 1, n_tok)
        scaled = (state * gain).astype(bf16)
        tile = min(256, ch)
        for j in range(0, ch, tile):
            part = jnp.dot(
                scaled, weight[:, pl.ds((1 - b) * ch + j, tile)], preferred_element_type=f32
            )
            s1[n][c, :, j : j + tile] = part.astype(s1[n].dtype)
        started(lambda d: pair_send(n, c), 0, 1)
        for j in range(0, ch, tile):
            acc[n][c, :, j : j + tile] = jnp.dot(
                scaled, weight[:, pl.ds(b * ch + j, tile)], preferred_element_type=f32
            )

    def scale_rows(k, c, total):
        each(1, n_tok, lambda d: squares_send(k, c, d).wait_recv())
        squares = sq_s[k, c]
        for d in range(1, n_tok):
            squares = squares + sq_r[k, c, d]
        inverse = lax.rsqrt(squares / width + epsilon)
        inv_ref[...] = jnp.broadcast_to(inverse[0:1, :], (128, rows)).T
        mine = inv_ref[pl.ds(z * rg, rg), :]
        return total * jnp.concatenate([mine] * (ch // 128), axis=1)

    def doc_sends():
        cols = pl.ds((1 - b) * ch, ch)
        return [
            to_tok(src, dst, kv_send.at[i], kv_recv.at[i], pair)
            for i, (src, dst) in enumerate(
                ((key_ref.at[:, cols], k2), (val_ref.at[:, cols], v2), (bias_ref, bias2))
            )
        ]

    def send_docs():
        for copy in doc_sends():
            copy.start()
        drains.append(lambda: [copy.wait_send() for copy in doc_sends()])

    def receive_docs():
        for copy in doc_sends():
            copy.wait_recv()
        biggest = jnp.zeros((1, 128), f32)
        for i, bias in enumerate((bias_ref, bias2)):
            mask[i] = jnp.broadcast_to(bias[0:1, :], (128, token_count)).T
            for hh in range(hh_n):
                if i == 0:
                    piece = val_ref[:, pl.ds(b * ch + hh * HS, HS)]
                else:
                    piece = v2[:, hh * HS : (hh + 1) * HS]
                piece = piece.astype(f32)
                biggest = jnp.maximum(biggest, jnp.max(jnp.abs(piece), axis=0, keepdims=True))
                vt[i, hh * HS : (hh + 1) * HS, :] = piece.T.astype(bf16)
        biggest = jnp.broadcast_to(jnp.max(biggest, axis=1, keepdims=True), (8, rows))
        for c in range(chunks):
            st_s[c, 2 * hh_n : 2 * hh_n + 8, :] = biggest

    def attend(c):
        for hh in range(hh_n):
            query = g[0][c, b, :, hh * HS : (hh + 1) * HS]
            parts = []
            for i in range(2):
                if i == 0:
                    keys = key_ref[:, pl.ds(b * ch + hh * HS, HS)]
                else:
                    keys = k2[:, hh * HS : (hh + 1) * HS]
                scores = lax.dot_general(
                    keys, query, (((1,), (1,)), ((), ())), preferred_element_type=f32
                ) * HS ** (-0.5)
                scores = jnp.where(
                    jnp.concatenate([mask[i]] * (rows // 128), axis=1) > 0.5, scores, masked_score
                )
                highest = jnp.max(scores, axis=0, keepdims=True)
                weights_b = jnp.exp(scores - highest)
                total = jnp.sum(weights_b, axis=0, keepdims=True)
                weighted = jnp.dot(
                    vt[i, hh * HS : (hh + 1) * HS, :], weights_b.astype(bf16),
                    preferred_element_type=f32,
                )
                parts.append((highest, total, weighted))
            (top_0, total_0, sum_0), (top_1, total_1, sum_1) = parts
            top = jnp.maximum(top_0, top_1)
            left, right = jnp.exp(top_0 - top), jnp.exp(top_1 - top)
            st_s[c, hh : hh + 1, :] = top
            st_s[c, hh_n + hh : hh_n + hh + 1, :] = left * total_0 + right * total_1
            wt[c, hh] = sum_0 * left + sum_1 * right
        started(functools.partial(stats_send, c), 1, nz)

    def normalise(c):
        each(1, nz, lambda d: stats_send(c, d).wait_recv())
        mine = st_s[c]
        top, biggest = mine[0:hh_n], mine[2 * hh_n :]
        for d in range(1, nz):
            top = jnp.maximum(top, st_r[c, d, 0:hh_n, :])
            biggest = jnp.maximum(biggest, st_r[c, d, 2 * hh_n :, :])
        own = jnp.exp(mine[0:hh_n] - top)
        den = own * mine[hh_n : 2 * hh_n]
        for d in range(1, nz):
            den = den + jnp.exp(st_r[c, d, 0:hh_n, :] - top) * st_r[c, d, hh_n : 2 * hh_n, :]
        factor = own / den
        biggest = jnp.maximum(biggest[0:1, 0:128], 1e-30)
        scale_ref[c, 0:1, :] = FULL / biggest
        scale_ref[c, 1:2, :] = biggest / FULL
        for hh in range(hh_n):
            part = (wt[c, hh] * factor[hh : hh + 1, :]).T
            acc[1][c, :, hh * HS : (hh + 1) * HS] = part
            s2[1][c, :, hh * HS : (hh + 1) * HS] = (
                jnp.round(part * scale_ref[c, 0:1, :]).astype(jnp.int32).astype(jnp.int16)
            )
        started(functools.partial(group_send, 1, c), 1, nz)

    def hpair_send(m, c):
        return to_head(
            h1s.at[m, c, pl.ds((1 - hb) * hr, hr), :], h1r.at[m, c],
            h_send.at[m, c, 0, 0], h_recv.at[m, c, 0, 0], hpair,
        )

    def hdirect_send(m, c, d):
        at = h2.at[m, c, hq]
        return to_head(
            at, at, h_send.at[m, c, 1, d], h_recv.at[m, c, 1, d], 2 * lax.rem(hq + d, nq) + hb
        )

    def hdirect_recv(m, c, d):
        at = h2.at[m, c, lax.rem(hq + nq - d, nq)]
        return to_head(
            at, at, h_send.at[m, c, 1, d], h_recv.at[m, c, 1, d], 2 * lax.rem(hq + d, nq) + hb
        )

    def hback(m, c, half):
        at = (state_ref if m == 0 else out_ref).at[pl.ds(c * rows + half * hr, hr), :]
        return to_head(at, at, h_send.at[m, c, 2, 0], h_recv.at[m, c, 2, 0], hpair)

    def head_partial(m, c, k, weight):
        tile = min(256, dt)
        left, right = g[k][c, 0], g[k][c, 1]
        for j in range(0, dt, tile):
            h1s[m, c, :, j : j + tile] = jnp.dot(
                left, weight[0:ch, j : j + tile], preferred_element_type=f32
            ) + jnp.dot(right, weight[ch : 2 * ch, j : j + tile], preferred_element_type=f32)
        started(lambda d: hpair_send(m, c), 0, 1)

    def head_pair(m, c):
        hpair_send(m, c).wait_recv()
        h2[m, c, hq] = h1s[m, c, pl.ds(hb * hr, hr), :] + h1r[m, c]
        started(functools.partial(hdirect_send, m, c), 1, nq)

    def head_total(m, c):
        each(1, nq, lambda d: hdirect_recv(m, c, d).wait_recv())
        total = h2[m, c, 0]
        for i in range(1, nq):
            total = total + h2[m, c, i]
        at = pl.ds(c * rows + hb * hr, hr)
        if m == 0:
            state_ref[at, :] = lat_ref[at, :] + total
        else:
            out_ref[at, :] = state_ref[at, :] + total
        started(lambda d: hback(m, c, hb), 0, 1)

    def head_back(m, c):
        hback(m, c, 1 - hb).wait_recv()

    def stage_0(c):
        if c == 0:
            send_docs()
            weights[0].wait()
        project(0, 0, c, lat_ref[c * rows : (c + 1) * rows, :], gain_ref[...], qw)

    def stage_2(c):
        sum_groups(0, c, lambda t: scale_rows(0, c, t).astype(bf16))

    def stage_4(c):
        if c == 0:
            receive_docs()
        each(1, nz, lambda d: share_recv(0, c, d).wait_recv())
        attend(c)

    def stage_9(c):
        if c == 0:
            weights[1].wait()
        gathered(1, c)
        head_partial(0, c, 1, ow)

    def stage_12(c):
        if c == 0:
            weights[2].wait()
        head_back(0, c)
        project(1, 2, c, state_ref[c * rows : (c + 1) * rows, :], mgain_ref[...], uw)

    def pair_2(c):
        sum_pair(2, c)

    def stage_14(c):
        sum_groups(2, c, lambda t: jax.nn.gelu(scale_rows(1, c, t)).astype(bf16))

    def stage_16(c):
        if c == 0:
            weights[3].wait()
        gathered(2, c)
        head_partial(1, c, 2, dw)

    stages = [
        stage_0,
        lambda c: sum_pair(0, c),
        stage_2,
        stage_4,
        normalise,
        lambda c: sum_groups(1, c, lambda t: t.astype(bf16)),
        lambda c: forward(1, c),
        stage_9,
        lambda c: head_pair(0, c),
        lambda c: head_total(0, c),
        stage_12,
        pair_2,
        stage_14,
        lambda c: forward(2, c),
        stage_16,
        lambda c: head_pair(1, c),
        lambda c: head_total(1, c),
        lambda c: head_back(1, c),
    ]
    for c in range(chunks):
        stages[0](c)
    for step in range(1, len(stages) + chunks - 1):
        for c in range(chunks):
            if 1 <= step - c < len(stages):
                stages[step - c](c)
    for drain in drains:
        drain()


def shards(
    n_tok, n_head, latents, doc_keys, doc_values, token_mask, shard_lengths,
    query_weight, output_weight, attn_gain, up_weight, down_weight, mlp_gain,
):
    token_count, features = doc_keys.shape
    latent_count, dt = latents.shape
    positions = jnp.arange(token_count, dtype=jnp.int32)
    valid = (token_mask == 1) & (positions < shard_lengths[0])
    bias = jnp.broadcast_to(valid.astype(f32)[None, :], (8, token_count))
    nz, nq = n_tok // 2, n_head // 2
    chunks = chunk_count(latent_count, nz)
    rows = latent_count // chunks
    rg, ch, hh_n = rows // nz, features // 2, features // (2 * HS)

    def per(make):
        return [make(t) for t in RS_TYPES]

    scratch = [
        pltpu.VMEM(query_weight.shape, bf16), pltpu.VMEM(output_weight.shape, bf16),
        pltpu.VMEM(up_weight.shape, bf16), pltpu.VMEM(down_weight.shape, bf16),
        pltpu.VMEM((2, ch, token_count), bf16),
        *per(lambda t: pltpu.VMEM((chunks, rows, ch), t)),
        *per(lambda t: pltpu.VMEM((chunks, rows, ch), t)),
        *per(lambda t: pltpu.VMEM((chunks, rows, ch), f32)),
        *per(lambda t: pltpu.VMEM((chunks, rows, ch) if t != f32 else (chunks + 1, 8, 128), t)),
        *per(lambda t: pltpu.VMEM((chunks, nz, rg, ch), t)),
        *per(lambda t: pltpu.VMEM((chunks, 2, rows, ch), bf16)),
        pltpu.VMEM((2, chunks, 8, rows), f32),
        pltpu.VMEM((2, chunks, n_tok, 8, rows), f32),
        pltpu.VMEM((chunks, 2 * hh_n + 8, rows), f32),
        pltpu.VMEM((chunks, nz, 2 * hh_n + 8, rows), f32),
        pltpu.VMEM((chunks, hh_n, HS, rows), f32),
        pltpu.VMEM((rows, 128), f32),
        pltpu.VMEM((token_count, ch), bf16),
        pltpu.VMEM((token_count, ch), bf16),
        pltpu.VMEM((8, token_count), f32),
        pltpu.VMEM((2, token_count, 128), f32),
        pltpu.VMEM((chunks, 8, 128), f32),
        pltpu.VMEM((2, chunks, rows, dt), f32),
        pltpu.VMEM((2, chunks, rows // 2, dt), f32),
        pltpu.VMEM((2, chunks, nq, rows // 2, dt), f32),
        pltpu.VMEM((latent_count, dt), f32),
        pltpu.SemaphoreType.DMA((4,)),
        pltpu.SemaphoreType.DMA((3, chunks, 4, nz)),
        pltpu.SemaphoreType.DMA((3, chunks, 4, nz)),
        pltpu.SemaphoreType.DMA((3, chunks, n_tok)),
        pltpu.SemaphoreType.DMA((3, chunks, n_tok)),
        pltpu.SemaphoreType.DMA((2, chunks, 3, nq)),
        pltpu.SemaphoreType.DMA((2, chunks, 3, nq)),
        pltpu.SemaphoreType.DMA((3,)),
        pltpu.SemaphoreType.DMA((3,)),
    ]
    vmem = pl.BlockSpec(memory_space=pltpu.VMEM)
    anywhere = pl.BlockSpec(memory_space=pl.ANY)
    return pl.pallas_call(
        functools.partial(kernel, n_tok, n_head, chunks, dt * n_tok),
        out_shape=jax.ShapeDtypeStruct(latents.shape, f32),
        in_specs=[vmem] * 6 + [anywhere] * 4,
        out_specs=vmem,
        scratch_shapes=scratch,
        compiler_params=pltpu.CompilerParams(
            collective_id=0, has_side_effects=True, vmem_limit_bytes=56 * 1024 * 1024
        ),
    )(
        latents, doc_keys, doc_values, bias, attn_gain[None, :], mlp_gain[None, :],
        query_weight, output_weight, up_weight, down_weight,
    )


def solution(mesh):
    in_specs = (
        P(None, "tok"),
        P("tok", "head"),
        P("tok", "head"),
        P("tok"),
        P("tok"),
        P("tok", "head"),
        P("head", "tok"),
        P("tok"),
        P("tok", "head"),
        P("head", "tok"),
        P("tok"),
    )
    return jax.shard_map(
        functools.partial(shards, mesh.shape["tok"], mesh.shape["head"]),
        mesh=mesh, in_specs=in_specs, out_specs=P(None, "tok"), check_vma=False,
    )
```
